256 devices in a mesh: pen: 128 (over y_hi, z, x, core), coil: 2 (over y_lo).
Axes of the slice: x: 4, y: 4 (y_hi: 2, y_lo: 2; y = y_hi * 2 + y_lo), z: 8, core: 2. Of those that a mesh axis runs over, the one named last changes fastest.
Arguments:
- image_field: float32 [512, 512, 2, 128], P('pen'), may hold values from -6 to 6
- coil_maps: bfloat16 [2, 512, 512, 2, 128], P('coil', 'pen'), may hold values from -5 to 5
- samples: bfloat16 [2, 4096, 128, 2, 128], P('coil', 'pen'), may hold values from -6 to 6
- kernels: bfloat16 [4096, 128, 128], P('pen'), may hold values from -0.5 to 0.5
- tile_of_block: int32 [4096], P('pen'), may hold values from 0 to 2047, as said below
Outputs:
- gradient: float32 [512, 512, 2, 128], P('pen', 'coil')
The draws below stay inside these ranges and needn't reach their ends.
Inputs may be any that keep to these rules, and one draw needn't show every extreme that they name: The tile of every block lies with the block: tile_of_block[b] // 16 == b // 32; every tile is named by at least one block.
All inputs are finite; a program needn't handle non-finite values.
Results may differ from the reference program's by a relative error of at most 0.012.
Values may be sent and summed in bfloat16 or wider, within the bound.
A program may use at most 128 MiB of HBM per device.

```python
import jax
import jax.numpy as jnp
from jax import lax

NL = 512
NZ = 128
TILE = 128
SAMP = 128
COILS = 2
LT = 16
TILES = 2048
BLK_DEV = 32
NBLK = 4096


def draw_tile_of_block(key, part):
    dev_count = NBLK // BLK_DEV
    first_key = jax.random.fold_in(key, 11)
    second_key = jax.random.fold_in(key, 12)
    base_tiles = jnp.tile(jnp.arange(LT, dtype=jnp.int32)[None, :], (dev_count, 1))
    extra_tiles = jax.random.randint(first_key, (dev_count, BLK_DEV - LT), 0, LT, dtype=jnp.int32)
    all_tiles = jnp.concatenate([base_tiles, extra_tiles], 1)
    key_list = jax.random.split(second_key, dev_count)
    shuffle = jax.vmap(lambda one_key: jax.random.permutation(one_key, BLK_DEV))(key_list)
    mixed = jnp.take_along_axis(all_tiles, shuffle.astype(jnp.int32), 1)
    owners = jnp.arange(dev_count, dtype=jnp.int32)[:, None] * LT
    return (mixed + owners).reshape(NBLK).astype(jnp.int32)


def shard_levels(stream_key, extent, cuts, least, top_value):
    def one(dim, shards_of):
        draws = jax.random.uniform(jax.random.fold_in(jax.random.fold_in(stream_key, 6), dim), (shards_of,), jnp.float32, least / len(cuts), top_value / len(cuts))
        return jnp.repeat(jnp.exp(draws), extent[dim] // shards_of).reshape((-1,) + (1,) * (len(extent) - dim - 1))

    gain = one(*cuts[0])
    for cut in cuts[1:]:
        gain = gain * one(*cut)
    return gain


def scatter_about(own_key, dims, deviation, limit, pieces=(), kind=jnp.bfloat16):
    level = shard_levels(own_key, dims, pieces, -0.22, 0.18) if pieces else 1.0
    array = jax.random.normal(own_key, dims, jnp.float32) * deviation * level
    return jnp.minimum(jnp.maximum(array, -limit), limit).astype(kind)


def setup_inputs(seed: int = 0) -> dict:
    keys = jax.random.split(jax.random.key(seed), 6)
    return {
        "image_field": scatter_about(keys[0], (NL, NL, 2, NZ), 1.0, 6.0, ((0, 128),), jnp.float32),
        "coil_maps": scatter_about(keys[1], (COILS, NL, NL, 2, NZ), 0.7, 5.0, ((0, 2), (1, 128))),
        "samples": scatter_about(keys[2], (COILS, NBLK, SAMP, 2, NZ), 1.0, 6.0, ((0, 2), (1, 128))),
        "kernels": scatter_about(keys[3], (NBLK, SAMP, TILE), TILE ** -0.5, 0.5, ((0, 128),)),
        "tile_of_block": draw_tile_of_block(jax.random.fold_in(keys[5], 71), 0),
    }


tv_weight = 2.0

def spectrum(real_part, imag_part, axis, inverse):
    values = lax.complex(real_part, imag_part)
    if inverse:
        result = jnp.fft.ifft(values, axis=axis, norm='ortho')
    else:
        result = jnp.fft.fft(values, axis=axis, norm='ortho')
    return (jnp.real(result), jnp.imag(result))

def to_tiles(field):
    return field.reshape(NL // TILE, TILE, NL, 2 * NZ).transpose(2, 0, 1, 3).reshape(TILES, TILE, 2 * NZ)

def from_tiles(tiles):
    return tiles.reshape(NL, NL // TILE, TILE, 2 * NZ).transpose(1, 2, 0, 3).reshape(NL, NL, 2, NZ)

def forward_diff(field, axis):
    count = field.shape[axis]
    head = lax.slice_in_dim(field, 1, count, axis=axis) - lax.slice_in_dim(field, 0, count - 1, axis=axis)
    return jnp.concatenate([head, jnp.zeros_like(lax.slice_in_dim(field, 0, 1, axis=axis))], axis)

def backward_take(flux, axis):
    count = flux.shape[axis]
    before = jnp.concatenate([jnp.zeros_like(lax.slice_in_dim(flux, 0, 1, axis=axis)), lax.slice_in_dim(flux, 0, count - 1, axis=axis)], axis)
    return before - flux

def tv_gradient(field):
    diff_y = forward_diff(field, 0)
    diff_x = forward_diff(field, 1)
    diff_z = forward_diff(field, 3)
    norm_den = jnp.sqrt(1.0 + lax.optimization_barrier(jnp.sum(diff_y * diff_y + diff_x * diff_x + diff_z * diff_z, axis=2, keepdims=True)))
    return backward_take(diff_y / norm_den, 0) + backward_take(diff_x / norm_den, 1) + backward_take(diff_z / norm_den, 3)

def reference(image_field, coil_maps, samples, kernels, tile_of_block):
    field_real = image_field[:, :, 0]
    field_imag = image_field[:, :, 1]
    groups = NBLK // BLK_DEV
    ker_groups = kernels.reshape(groups, BLK_DEV, SAMP, TILE)
    id_groups = tile_of_block.reshape(groups, BLK_DEV)
    summed = jnp.zeros(image_field.shape, jnp.float32)
    for coil_idx in range(COILS):
        map_real = coil_maps[coil_idx, :, :, 0].astype(jnp.float32)
        map_imag = coil_maps[coil_idx, :, :, 1].astype(jnp.float32)
        coil_real = (map_real * field_real - map_imag * field_imag).astype(jnp.bfloat16)
        coil_imag = (map_real * field_imag + map_imag * field_real).astype(jnp.bfloat16)
        spec_real, spec_imag = spectrum(coil_real.astype(jnp.float32), coil_imag.astype(jnp.float32), 1, False)
        spec_real = spec_real.astype(jnp.bfloat16).astype(jnp.float32)
        spec_imag = spec_imag.astype(jnp.bfloat16).astype(jnp.float32)
        grid_real, grid_imag = spectrum(spec_real, spec_imag, 0, False)
        kspace_grid = jnp.stack([grid_real, grid_imag], 2).astype(jnp.bfloat16)
        grid_tiles = to_tiles(kspace_grid)
        sample_groups = samples[coil_idx].reshape(groups, BLK_DEV, SAMP, 2 * NZ)

        def add_group(carry, group):
            ker_block, id_block, sample_block = group
            ker_wide = ker_block.astype(jnp.float32)
            picked = grid_tiles[id_block].astype(jnp.float32)
            predicted = jnp.einsum('bst,btc->bsc', ker_wide, picked)
            misfit = (predicted - sample_block.astype(jnp.float32)).astype(jnp.bfloat16)
            back_terms = jnp.einsum('bst,bsc->btc', ker_wide, misfit.astype(jnp.float32))
            return (carry.at[id_block].add(back_terms), None)
        back_tiles, unused = lax.scan(add_group, jnp.zeros((TILES, TILE, 2 * NZ), jnp.float32), (ker_groups, id_groups, sample_groups))
        back_grid = from_tiles(back_tiles.astype(jnp.bfloat16)).astype(jnp.float32)
        rows_real, rows_imag = spectrum(back_grid[:, :, 0], back_grid[:, :, 1], 0, True)
        rows_real = rows_real.astype(jnp.bfloat16).astype(jnp.float32)
        rows_imag = rows_imag.astype(jnp.bfloat16).astype(jnp.float32)
        back_real, back_imag = spectrum(rows_real, rows_imag, 1, True)
        summed = summed + jnp.stack([map_real * back_real + map_imag * back_imag, map_real * back_imag - map_imag * back_real], 2)
    return summed + tv_weight * tv_gradient(image_field)
```

```python
import math

import jax
import jax.numpy as jnp
from jax import lax
from jax.experimental import pallas as pl
from jax.experimental.pallas import tpu as pltpu
from jax.sharding import PartitionSpec as P

NL = 512
NZ = 128
TILE = 128


tv_weight = 2.0


def shifted(shard, axis, by):
    length = lax.axis_size(axis)
    pairs = [(i, i + by) for i in range(length) if 0 <= i + by < length]
    return lax.ppermute(shard, axis, pairs)


def exchange_kernel(blocks_ref, out_ref, send_sem, recv_sem, own_sem):
    me = lax.axis_index("pen")
    coil = lax.axis_index("coil")
    y, z, rest = me // 64, me // 8 % 8, me % 8

    def partner(i):
        step = i + 1
        dz, other = step % 8, step // 8
        return (y + other // 8) % 2 * 64 + (z + dz) % 8 * 8 + (rest + other % 8) % 8

    barrier = pltpu.get_barrier_semaphore()

    def greet(i, carry):
        pl.semaphore_signal(
            barrier, inc=1, device_id=(partner(i), coil), device_id_type=pl.DeviceIdType.MESH
        )
        return carry

    lax.fori_loop(0, 127, greet, 0)
    own = pltpu.make_async_copy(blocks_ref.at[me], out_ref.at[me], own_sem)
    own.start()
    pl.semaphore_wait(barrier, 127)

    def send(i, carry):
        d = partner(i)
        pltpu.make_async_remote_copy(
            blocks_ref.at[d],
            out_ref.at[me],
            send_sem,
            recv_sem,
            device_id=(d, coil),
            device_id_type=pl.DeviceIdType.MESH,
        ).start()
        return carry

    lax.fori_loop(0, 127, send, 0)
    own.wait()
    part = out_ref.at[pl.ds(0, 127)]
    pltpu.make_async_copy(part, part, recv_sem).wait()
    pltpu.make_async_copy(part, part, send_sem).wait()


def exchange(blocks):
    return pl.pallas_call(
        exchange_kernel,
        out_shape=jax.ShapeDtypeStruct(blocks.shape, blocks.dtype),
        in_specs=[pl.BlockSpec(memory_space=pltpu.VMEM)],
        out_specs=pl.BlockSpec(memory_space=pltpu.VMEM),
        scratch_shapes=[pltpu.SemaphoreType.DMA] * 3,
        compiler_params=pltpu.CompilerParams(collective_id=0, has_side_effects=True),
    )(blocks)


def dft_tables(length, direction):
    index = lax.iota(jnp.int32, length)
    phase = index[:, None] * index[None, :] % length
    angle = 2.0 * math.pi / length * phase.astype(jnp.float32)
    cosine = jnp.cos(angle) / math.sqrt(length)
    sine = direction * jnp.sin(angle) / math.sqrt(length)
    table = jnp.stack([jnp.stack([cosine, sine], -1), jnp.stack([-sine, cosine], -1)], 1)
    high_part = table.astype(jnp.bfloat16)
    low_part = (table - high_part.astype(jnp.float32)).astype(jnp.bfloat16)
    return (high_part, low_part)


def along_second(tables, values):
    first = jnp.einsum("kpxr,yxrz->ykpz", tables[0], values, preferred_element_type=jnp.float32)
    return first + jnp.einsum(
        "kpxr,yxrz->ykpz", tables[1], values, preferred_element_type=jnp.float32
    )


def along_first(tables, values):
    first = jnp.einsum("kpyr,yxrz->kxpz", tables[0], values, preferred_element_type=jnp.float32)
    return first + jnp.einsum(
        "kpyr,yxrz->kxpz", tables[1], values, preferred_element_type=jnp.float32
    )


def flux_fields(extended, first_row, first_col):
    center = extended[:-1, :-1]
    row_ids = first_row + jnp.arange(center.shape[0])
    col_ids = first_col + jnp.arange(center.shape[1])
    diff_y = (extended[1:, :-1] - center) * (row_ids != NL - 1)[:, None, None, None]
    diff_x = (extended[:-1, 1:] - center) * (col_ids != NL - 1)[None, :, None, None]
    diff_z = jnp.concatenate(
        [center[..., 1:] - center[..., :-1], jnp.zeros_like(center[..., :1])], 3
    )
    norm_den = jnp.sqrt(
        1.0 + jnp.sum(diff_y * diff_y + diff_x * diff_x + diff_z * diff_z, axis=2, keepdims=True)
    )
    inside = ((row_ids >= 0)[:, None] & (col_ids >= 0)[None, :]).astype(jnp.float32)[
        :, :, None, None
    ]
    return (diff_y / norm_den * inside, diff_x / norm_den * inside, diff_z / norm_den * inside)


def plane_divergence(flux_z):
    return jnp.concatenate([jnp.zeros_like(flux_z[..., :1]), flux_z[..., :-1]], 3) - flux_z


def on_device(image_field, coil_maps, samples, kernels, tile_of_block):
    own_rows = image_field.shape[0]
    pen_count = lax.axis_size("pen")
    half_cols = NL // lax.axis_size("coil")
    local_cols = NL // pen_count
    pen_id = lax.axis_index("pen")
    coil_id = lax.axis_index("coil")
    row_start = pen_id * own_rows
    col_start = coil_id * half_cols
    map_real = coil_maps[0, :, :, 0].astype(jnp.float32)
    map_imag = coil_maps[0, :, :, 1].astype(jnp.float32)
    field_real = image_field[:, :, 0]
    field_imag = image_field[:, :, 1]
    coil_image = jnp.stack(
        [
            map_real * field_real - map_imag * field_imag,
            map_real * field_imag + map_imag * field_real,
        ],
        2,
    ).astype(jnp.bfloat16)
    forward_tab = dft_tables(NL, 1.0)
    adjoint_tab = dft_tables(NL, -1.0)
    rows_spectrum = along_second(forward_tab, coil_image).astype(jnp.bfloat16)
    kspace_grid = along_first(
        forward_tab, exchange(
            rows_spectrum.reshape(4, 128, 4, 256).transpose(1, 0, 2, 3).reshape(128, 16, 256)
        ).reshape(512, 4, 2, 128)
    ).astype(jnp.bfloat16)
    grid_tiles = (
        kspace_grid.reshape(NL // TILE, TILE, local_cols, 2 * NZ)
        .transpose(2, 0, 1, 3)
        .reshape(-1, TILE, 2 * NZ)
    )
    tile_count = grid_tiles.shape[0]
    local_ids = tile_of_block - pen_id * tile_count
    picked = jnp.take(grid_tiles, local_ids, axis=0)
    predicted = jnp.einsum("bst,btc->bsc", kernels, picked, preferred_element_type=jnp.float32)
    measured = samples[0].reshape(predicted.shape).astype(jnp.float32)
    misfit = (predicted - measured).astype(jnp.bfloat16)
    back_terms = jnp.einsum("bst,bsc->btc", kernels, misfit, preferred_element_type=jnp.float32)
    onehot = (local_ids[:, None] == jnp.arange(tile_count, dtype=jnp.int32)[None, :]).astype(
        jnp.float32
    )
    back_tiles = jnp.einsum(
        "bl,btc->ltc", onehot, back_terms, precision=lax.Precision.HIGHEST
    ).astype(jnp.bfloat16)
    back_grid = (
        back_tiles.reshape(local_cols, NL // TILE, TILE, 2 * NZ)
        .transpose(1, 2, 0, 3)
        .reshape(NL, local_cols, 2, NZ)
    )
    back_rows = along_first(adjoint_tab, back_grid).astype(jnp.bfloat16)
    back_image = along_second(
        adjoint_tab, exchange(back_rows.reshape(128, 16, 256))
        .reshape(128, 4, 4, 256)
        .transpose(1, 0, 2, 3)
        .reshape(4, 512, 2, 128)
    )
    back_real = back_image[:, :, 0]
    back_imag = back_image[:, :, 1]
    coil_term = jnp.stack(
        [map_real * back_real + map_imag * back_imag, map_real * back_imag - map_imag * back_real],
        2,
    )
    summed = lax.psum(coil_term, "coil")
    data_gradient = lax.dynamic_slice_in_dim(summed, col_start, half_cols, 1)
    padded = jnp.pad(image_field, ((0, 0), (1, 1), (0, 0), (0, 0)))
    window = lax.dynamic_slice_in_dim(padded, col_start, half_cols + 2, 1)
    upper_row = shifted(window[:1], "pen", -1)
    extended = jnp.concatenate([window, upper_row], 0)
    flux_y, flux_x, flux_z = flux_fields(extended, row_start, col_start - 1)
    lower_row = shifted(flux_y[-1:], "pen", 1)
    flux_before = jnp.concatenate([lower_row, flux_y[:-1]], 0)
    tv_part = (
        flux_before[:, 1:]
        - flux_y[:, 1:]
        + flux_x[:, :-1]
        - flux_x[:, 1:]
        + plane_divergence(flux_z[:, 1:])
    )
    return data_gradient + tv_weight * tv_part


def solution(mesh):
    in_specs = (
        P("pen", None, None, None),
        P("coil", "pen", None, None, None),
        P("coil", "pen", None, None, None),
        P("pen", None, None),
        P("pen"),
    )
    out_specs = P("pen", "coil", None, None)
    return jax.shard_map(
        on_device, mesh=mesh, in_specs=in_specs, out_specs=out_specs, check_vma=False
    )
```

```python
import numpy as np

import jax
import jax.numpy as jnp
from jax import lax
from jax.experimental import pallas as pl
from jax.experimental.pallas import tpu as pltpu
from jax.sharding import PartitionSpec as P

NL = 512
NZ = 128
TILE = 128
PENS = 128
ROWS = 4
BLOCKS = 32
TILES = 16
HALF = NL // 2
PAD = 8
TV_WEIGHT = 2.0
MESH = pl.DeviceIdType.MESH


def dft_table():
    index = np.arange(NL)
    angle = 2.0 * np.pi / NL * (index[:, None] * index[None, :] % NL)
    return np.concatenate([np.cos(angle), np.sin(angle)], 1).astype(jnp.bfloat16)


def split_table():
    table = np.zeros((256, 256), np.float32)
    index = np.arange(128)
    table[index, 2 * index] = 1.0
    table[128 + index, 2 * index + 1] = 1.0
    return table.astype(jnp.bfloat16)


def low_lanes(shape):
    return lax.broadcasted_iota(jnp.int32, shape, len(shape) - 1) < 64


def swap(value):
    return pltpu.roll(value, 64, 1)


def matmul(left, right):
    return jnp.dot(left, right, preferred_element_type=jnp.float32)


def to_messages(result):
    count = result.shape[0] // 8
    groups = [result[:, 128 * a : 128 * (a + 1)].reshape(count, 8, 128) for a in range(4)]
    upper = lax.broadcasted_iota(jnp.int32, (count, 8, 128), 1) < 4
    even, odd = [], []
    for a in (0, 2):
        first, second = groups[a], groups[a + 1]
        even.append(jnp.where(upper, first, pltpu.roll(second, 4, 1)))
        odd.append(jnp.where(upper, pltpu.roll(first, 4, 1), second))
    both = jnp.stack([jnp.concatenate(even, 1), jnp.concatenate(odd, 1)], 1)
    return both.reshape(2 * count, 16, 128).astype(jnp.bfloat16)


def body(
    links,
    image_hbm,
    maps_hbm,
    samples_hbm,
    kernels_hbm,
    table_hbm,
    split_hbm,
    out_ref,
    image,
    maps,
    samples,
    kernels,
    table,
    split,
    planes,
    map_real,
    map_imag,
    packed,
    send_fwd,
    recv_fwd,
    send_back,
    recv_back,
    history,
    gram,
    target,
    wide,
    own_term,
    send_term,
    recv_term,
    tv_part,
    load_sem,
    own_sem,
    fwd_send_sem,
    fwd_recv_sem,
    back_send_sem,
    back_recv_sem,
    term_send_sem,
    term_recv_sem,
    halo_send_sem,
    halo_recv_sem,
):
    me = lax.axis_index("pen")
    coil = lax.axis_index("coil")
    other = 1 - coil
    y, z, rest = me // 64, me // 8 % 8, me % 8

    def partner(i):
        step = i + 1
        dz, more = step % 8, step // 8
        return (y + more // 8) % 2 * 64 + (z + dz) % 8 * 8 + (rest + more % 8) % 8

    pairs = (
        (image_hbm, image),
        (maps_hbm, maps),
        (split_hbm, split),
        (table_hbm, table),
        (kernels_hbm, kernels),
        (samples_hbm, samples),
    )
    loads = [pltpu.make_async_copy(a, b, load_sem.at[i]) for i, (a, b) in enumerate(pairs)]
    for load in loads:
        load.start()

    barrier = pltpu.get_barrier_semaphore()

    def greet(i, carry):
        pl.semaphore_signal(barrier, inc=1, device_id=(partner(i), coil), device_id_type=MESH)
        return carry

    lax.fori_loop(0, PENS - 1, greet, 0)
    pl.semaphore_signal(barrier, inc=1, device_id=(me, other), device_id_type=MESH)

    for load in loads[:3]:
        load.wait()
    planes[:, 1 : ROWS + 1, 0:PAD, :] = jnp.zeros((2, ROWS, PAD, NZ), jnp.float32)
    planes[:, 1 : ROWS + 1, PAD + NL :, :] = jnp.zeros((2, ROWS, PAD, NZ), jnp.float32)

    def coil_block(i, carry):
        row, part = i // 4, i % 4
        start = pl.multiple_of(part * 128, 128)
        low = low_lanes((128, 128))
        pieces = matmul(split[...], maps[row, pl.ds(pl.multiple_of(part * 256, 256), 256), :])
        pieces = pieces * (1.0 / NL)
        real, imag = pieces[:128], pieces[128:]
        real_sw, imag_sw = swap(real), swap(imag)
        field = image.at[row, pl.ds(pl.multiple_of(part * 256, 256), 256), :]
        f_real, f_imag = field[pl.ds(0, 128, 2), :], field[pl.ds(1, 128, 2), :]
        planes[0, row + 1, pl.ds(start + PAD, 128), :] = f_real
        planes[1, row + 1, pl.ds(start + PAD, 128), :] = f_imag
        f_real_sw, f_imag_sw = swap(f_real), swap(f_imag)
        by_half = (
            (jnp.where(low, real, real_sw), jnp.where(low, imag, -imag_sw), jnp.where(low, f_real, f_imag_sw), jnp.where(low, f_imag, f_real_sw)),
            (jnp.where(low, real_sw, real), jnp.where(low, imag_sw, -imag), jnp.where(low, f_real_sw, f_imag), jnp.where(low, f_imag_sw, f_real)),
        )
        for half, (m_real, m_imag, f, f_sw) in enumerate(by_half):
            map_real[half, row, pl.ds(start, 128), :] = m_real.astype(jnp.bfloat16)
            map_imag[half, row, pl.ds(start, 128), :] = m_imag.astype(jnp.bfloat16)
            value = m_real * f - m_imag * f_sw
            turned = swap(value)
            lanes = pl.ds(pl.multiple_of(row * 128, 128), 128)
            packed[half, pl.ds(start, 128), lanes] = value.astype(jnp.bfloat16)
            packed[half, pl.ds(start + NL, 128), lanes] = jnp.where(low, turned, -turned).astype(jnp.bfloat16)
        return carry

    lax.fori_loop(0, 16, coil_block, 0)
    loads[3].wait()

    def to_send(half, send):
        def step(i, carry):
            rows = pl.ds(pl.multiple_of(i * 256, 256), 256)
            send[half, pl.ds(i * 64, 64)] = to_messages(matmul(table[rows, :], packed[half]))
            return carry

        lax.fori_loop(0, 2, step, 0)

    def post(half, send, recv, send_sem, recv_sem, own_index):
        def step(i, carry):
            d = partner(i)
            pltpu.make_async_remote_copy(
                send.at[half, d],
                recv.at[half, me],
                send_sem.at[half],
                recv_sem.at[half],
                device_id=(d, coil),
                device_id_type=MESH,
            ).start()
            return carry

        own = pltpu.make_async_copy(send.at[half, me], recv.at[half, me], own_sem.at[own_index])
        own.start()
        lax.fori_loop(0, PENS - 1, step, 0)
        return own

    def await_all(half, ref, sem):
        part = ref.at[half, pl.ds(0, PENS - 1)]
        pltpu.make_async_copy(part, part, sem.at[half]).wait()

    def unpack(half, recv, sign):
        def widen(i, carry):
            wide[pl.ds(pl.multiple_of(i * 256, 256), 256), :] = (
                recv[half, pl.ds(i * 16, 16)].reshape(256, 128).astype(jnp.float32)
            )
            return carry

        lax.fori_loop(0, 8, widen, 0)
        low = low_lanes((128, 128))
        for a in range(4):
            for part in range(4):
                value = wide[pl.ds(a + 512 * part, 128, 4), :]
                turned = swap(value) * sign
                lanes = slice(a * 128, a * 128 + 128)
                packed[half, 128 * part : 128 * part + 128, lanes] = value.astype(jnp.bfloat16)
                packed[half, NL + 128 * part : NL + 128 * part + 128, lanes] = jnp.where(
                    low, turned, -turned
                ).astype(jnp.bfloat16)

    to_send(0, send_fwd)
    pl.semaphore_wait(barrier, PENS)
    own0 = post(0, send_fwd, recv_fwd, fwd_send_sem, fwd_recv_sem, 0)
    to_send(1, send_fwd)
    own1 = post(1, send_fwd, recv_fwd, fwd_send_sem, fwd_recv_sem, 1)

    window = pl.ds(pl.multiple_of(coil * HALF, HALF), HALF + 2 * PAD)
    halos = []
    for i, (source, place, to) in enumerate(((1, ROWS + 1, me + PENS - 1), (ROWS, 0, me + 1))):
        halo = pltpu.make_async_remote_copy(
            planes.at[:, source, window],
            planes.at[:, place, window],
            halo_send_sem.at[i],
            halo_recv_sem.at[i],
            device_id=(to % PENS, coil),
            device_id_type=MESH,
        )
        halo.start()
        halos.append(halo)

    loads[4].wait()
    loads[5].wait()
    history[0] = jnp.zeros((TILE, 3 * 128), jnp.float32)

    def chain(i, carry):
        weights = kernels[i]
        pieces = matmul(split[...], samples[i]).astype(jnp.bfloat16)
        right = jnp.concatenate([weights, pieces[:128], pieces[128:]], 1)
        term = lax.dot_general(weights, right, (((0,), (0,)), ((), ())), preferred_element_type=jnp.float32)
        history[i + 1] = history[links[i]] + term
        return carry

    lax.fori_loop(0, BLOCKS, chain, 0)

    def finish(tile, carry):
        total = history[links[BLOCKS + tile]]
        low = low_lanes((128, 128))
        gram[tile] = total[:, :128].astype(jnp.bfloat16)
        real, imag = total[:, 128:256], total[:, 256:]
        target[0, tile] = jnp.where(low, real, swap(imag))
        target[1, tile] = jnp.where(low, swap(real), imag)
        return carry

    lax.fori_loop(0, TILES, finish, 0)

    def grid_side(half, own):
        await_all(half, recv_fwd, fwd_recv_sem)
        own.wait()
        unpack(half, recv_fwd, 1.0)
        low = low_lanes((128, 128))
        spectrum = []
        for i in range(2):
            spectrum.append(matmul(table[256 * i : 256 * i + 256, :], packed[half]).astype(jnp.bfloat16))
        for i in range(2):
            for k in range(2):
                quarter = 2 * i + k
                for column in range(4):
                    lanes = slice(column * 128, column * 128 + 128)
                    cells = spectrum[i][128 * k : 128 * k + 128, lanes]
                    tile = 4 * column + quarter
                    value = matmul(gram[tile], cells) - target[half, tile]
                    turned = swap(value)
                    packed[half, 128 * quarter : 128 * quarter + 128, lanes] = value.astype(jnp.bfloat16)
                    packed[half, NL + 128 * quarter : NL + 128 * quarter + 128, lanes] = jnp.where(
                        low, -turned, turned
                    ).astype(jnp.bfloat16)
        to_send(half, send_back)
        return post(half, send_back, recv_back, back_send_sem, back_recv_sem, 2 + half)

    own2 = grid_side(0, own0)

    for halo in halos:
        halo.wait_recv()
    first_col = coil * HALF

    def tv_columns(i, carry):
        lane = lax.broadcasted_iota(jnp.int32, (72, 128), 1)
        cols = lax.broadcasted_iota(jnp.int32, (72, 128), 0) + (first_col + i * 64 - PAD)
        col_ok = jnp.logical_and(cols >= 0, cols != NL - 1)
        start = pl.multiple_of(first_col + i * 64, 64)

        def tv_row(k, before):
            row = me * ROWS + k - 1
            row_ok = jnp.logical_and(row >= 0, row != NL - 1).astype(jnp.float32)
            diffs, squares = [], 1.0
            for r in range(2):
                here = planes[r, k, pl.ds(start, 80), :]
                above = planes[r, k + 1, pl.ds(start, 72), :]
                center = here[:72]
                diff_y = (above - center) * row_ok
                diff_x = jnp.where(col_ok, here[1:73] - center, 0.0)
                diff_z = jnp.where(lane == NZ - 1, 0.0, pltpu.roll(center, NZ - 1, 1) - center)
                squares = squares + (diff_y * diff_y + diff_x * diff_x + diff_z * diff_z)
                diffs.append((diff_y, diff_x, diff_z))
            inverse = TV_WEIGHT / jnp.sqrt(squares)
            after = []
            for r in range(2):
                flux_y, flux_x, flux_z = (diff * inverse for diff in diffs[r])
                flux_y, flux_z = flux_y[8:], flux_z[8:]
                shifted = jnp.where(lane[8:] == 0, 0.0, pltpu.roll(flux_z, 1, 1))
                tv_part[k, r, pl.ds(pl.multiple_of(i * 64, 64), 64), :] = (
                    before[r] - flux_y + flux_x[7:71] - flux_x[8:] + shifted - flux_z
                )
                after.append(flux_y)
            return tuple(after)

        zero = jnp.zeros((64, 128), jnp.float32)
        lax.fori_loop(0, ROWS + 1, tv_row, (zero, zero))
        return carry

    lax.fori_loop(0, HALF // 64, tv_columns, 0)

    own3 = grid_side(1, own1)

    def coil_terms(half, side):
        columns = pl.ds(pl.multiple_of(side * HALF, HALF), HALF)
        result = matmul(table[columns, :], packed[half])
        for row in range(ROWS):
            value = result[:, row * 128 : row * 128 + 128]
            real = map_real[half, row, columns, :].astype(jnp.float32)
            imag = map_imag[half, row, columns, :].astype(jnp.float32)
            yield row, real * value + imag * swap(value)

    def image_side(half, own):
        await_all(half, recv_back, back_recv_sem)
        own.wait()
        unpack(half, recv_back, -1.0)
        for row, term in coil_terms(half, other):
            send_term[half, row] = term.astype(jnp.bfloat16)
        copy = pltpu.make_async_remote_copy(
            send_term.at[half],
            recv_term.at[half],
            term_send_sem.at[half],
            term_recv_sem.at[half],
            device_id=(me, other),
            device_id_type=MESH,
        )
        copy.start()
        for row, term in coil_terms(half, coil):
            own_term[half, row] = term
        return copy

    copies = [image_side(0, own2), image_side(1, own3)]
    for halo in halos:
        halo.wait_send()
    for half in range(2):
        await_all(half, send_fwd, fwd_send_sem)
        await_all(half, send_back, back_send_sem)
    for copy in copies:
        copy.wait()

    def combine(row, carry):
        low = low_lanes((HALF, 128))
        first = own_term[0, row] + recv_term[0, row].astype(jnp.float32)
        second = own_term[1, row] + recv_term[1, row].astype(jnp.float32)
        out_ref[row, pl.ds(0, HALF, 2), :] = jnp.where(low, first, swap(second)) + tv_part[row + 1, 0]
        out_ref[row, pl.ds(1, HALF, 2), :] = jnp.where(low, swap(first), second) + tv_part[row + 1, 1]
        return carry

    lax.fori_loop(0, ROWS, combine, 0)


def on_device(image_field, coil_maps, samples, kernels, tile_of_block):
    ids = tile_of_block % TILES
    place = jnp.arange(BLOCKS, dtype=jnp.int32)
    wanted = jnp.concatenate([ids, jnp.arange(TILES, dtype=jnp.int32)])
    limit = jnp.minimum(jnp.arange(BLOCKS + TILES, dtype=jnp.int32), BLOCKS)
    hits = jnp.logical_and(wanted[:, None] == ids[None, :], place[None, :] < limit[:, None])
    links = jnp.max(jnp.where(hits, place[None, :] + 1, 0), axis=1)
    bf16, f32 = jnp.bfloat16, jnp.float32
    dma = pltpu.SemaphoreType.DMA
    hbm = pl.BlockSpec(memory_space=pl.ANY)
    out = pl.pallas_call(
        body,
        out_shape=jax.ShapeDtypeStruct((ROWS, 2 * HALF, NZ), f32),
        in_specs=[pl.BlockSpec(memory_space=pltpu.SMEM)] + [hbm] * 6,
        out_specs=pl.BlockSpec(memory_space=pltpu.VMEM),
        scratch_shapes=[
            pltpu.VMEM((ROWS, 2 * NL, NZ), f32),
            pltpu.VMEM((ROWS, 2 * NL, NZ), bf16),
            pltpu.VMEM((BLOCKS, 256, NZ), bf16),
            pltpu.VMEM((BLOCKS, TILE, TILE), bf16),
            pltpu.VMEM((NL, 2 * NL), bf16),
            pltpu.VMEM((256, 256), bf16),
            pltpu.VMEM((2, ROWS + 2, NL + 2 * PAD, NZ), f32),
            pltpu.VMEM((2, ROWS, NL, NZ), bf16),
            pltpu.VMEM((2, ROWS, NL, NZ), bf16),
            pltpu.VMEM((2, 2 * NL, 4 * 128), bf16),
            pltpu.VMEM((2, PENS, 16, 128), bf16),
            pltpu.VMEM((2, PENS, 16, 128), bf16),
            pltpu.VMEM((2, PENS, 16, 128), bf16),
            pltpu.VMEM((2, PENS, 16, 128), bf16),
            pltpu.VMEM((BLOCKS + 1, TILE, 3 * 128), f32),
            pltpu.VMEM((TILES, TILE, TILE), bf16),
            pltpu.VMEM((2, TILES, TILE, 128), f32),
            pltpu.VMEM((PENS * 16, 128), f32),
            pltpu.VMEM((2, ROWS, HALF, 128), f32),
            pltpu.VMEM((2, ROWS, HALF, 128), bf16),
            pltpu.VMEM((2, ROWS, HALF, 128), bf16),
            pltpu.VMEM((ROWS + 1, 2, HALF, 128), f32),
            dma((6,)),
            dma((4,)),
            dma((2,)),
            dma((2,)),
            dma((2,)),
            dma((2,)),
            dma((2,)),
            dma((2,)),
            dma((2,)),
            dma((2,)),
        ],
        compiler_params=pltpu.CompilerParams(
            collective_id=0, has_side_effects=True, vmem_limit_bytes=56 << 20
        ),
        name="adjoint_gradient",
    )(
        links,
        image_field.reshape(ROWS, 2 * NL, NZ),
        coil_maps.reshape(ROWS, 2 * NL, NZ),
        samples.reshape(BLOCKS, 256, NZ),
        kernels,
        jnp.asarray(dft_table()),
        jnp.asarray(split_table()),
    )
    return out.reshape(ROWS, HALF, 2, NZ)


def solution(mesh):
    in_specs = (
        P("pen", None, None, None),
        P("coil", "pen", None, None, None),
        P("coil", "pen", None, None, None),
        P("pen", None, None),
        P("pen"),
    )
    out_specs = P("pen", "coil", None, None)
    return jax.shard_map(
        on_device, mesh=mesh, in_specs=in_specs, out_specs=out_specs, check_vma=False
    )
```

```python
import numpy as np

import jax
import jax.numpy as jnp
from jax import lax
from jax.experimental import pallas as pl
from jax.experimental.pallas import tpu as pltpu
from jax.sharding import PartitionSpec as P

NL = 512
NZ = 128
TILE = 128
PENS = 128
ROWS = 4
BLOCKS = 32
TILES = 16
HALF = NL // 2
PAD = 8
TV_WEIGHT = 2.0
MESH = pl.DeviceIdType.MESH


def dft_table():
    index = np.arange(NL)
    angle = 2.0 * np.pi / NL * (index[:, None] * index[None, :] % NL)
    return np.concatenate([np.cos(angle), np.sin(angle)], 1).astype(jnp.bfloat16)


def split_table():
    table = np.zeros((256, 256), np.float32)
    index = np.arange(128)
    table[index, 2 * index] = 1.0
    table[128 + index, 2 * index + 1] = 1.0
    return table.astype(jnp.bfloat16)


def low_lanes(shape):
    return lax.broadcasted_iota(jnp.int32, shape, len(shape) - 1) < 64


def swap(value):
    return pltpu.roll(value, 64, 1)


def matmul(left, right):
    return jnp.dot(left, right, preferred_element_type=jnp.float32)


def to_messages(result):
    count = result.shape[0] // 8
    groups = [result[:, 128 * a : 128 * (a + 1)].reshape(count, 8, 128) for a in range(4)]
    upper = lax.broadcasted_iota(jnp.int32, (count, 8, 128), 1) < 4
    even, odd = [], []
    for a in (0, 2):
        first, second = groups[a], groups[a + 1]
        even.append(jnp.where(upper, first, pltpu.roll(second, 4, 1)))
        odd.append(jnp.where(upper, pltpu.roll(first, 4, 1), second))
    both = jnp.stack([jnp.concatenate(even, 1), jnp.concatenate(odd, 1)], 1)
    return both.reshape(2 * count, 16, 128).astype(jnp.bfloat16)


def body(
    tile_ids,
    image_hbm,
    maps_hbm,
    samples_hbm,
    kernels_hbm,
    table_hbm,
    split_hbm,
    data_out,
    tv_out,
    image,
    maps,
    samples,
    kernels,
    table,
    split,
    planes,
    map_real,
    map_imag,
    packed,
    send_fwd,
    recv_fwd,
    send_back,
    recv_back,
    history,
    gram,
    target,
    wide,
    own_term,
    send_term,
    recv_term,
    tv_part,
    data_part,
    links_vector,
    links,
    load_sem,
    own_sem,
    fwd_send_sem,
    fwd_recv_sem,
    back_send_sem,
    back_recv_sem,
    term_send_sem,
    term_recv_sem,
    store_sem,
    halo_send_sem,
    halo_recv_sem,
    links_sem,
):
    me = lax.axis_index("pen")
    coil = lax.axis_index("coil")
    other = 1 - coil
    y, z, rest = me // 64, me // 8 % 8, me % 8
    ring = [(z + d) % 8 * 8 for d in (4, 3, 5, 2, 6, 1, 7, 0)]

    def for_partners(act):
        def group(i, carry):
            base = (y + 1 - i // 8) % 2 * 64 + (rest + 15 - i) % 8
            for place in ring:
                act(base + place)
            return carry

        lax.fori_loop(0, 15, group, 0)
        for place in ring[:7]:
            act(y * 64 + rest + place)

    pairs = (
        (image_hbm, image),
        (maps_hbm, maps),
        (split_hbm, split),
        (table_hbm, table),
        (kernels_hbm, kernels),
        (samples_hbm, samples),
    )
    loads = [pltpu.make_async_copy(a, b, load_sem.at[i]) for i, (a, b) in enumerate(pairs)]
    for load in loads:
        load.start()

    barrier = pltpu.get_barrier_semaphore()

    def greet(d):
        pl.semaphore_signal(barrier, inc=1, device_id=(d, coil), device_id_type=MESH)

    for_partners(greet)
    pl.semaphore_signal(barrier, inc=1, device_id=(me, other), device_id_type=MESH)

    ids = jnp.broadcast_to(tile_ids[...] % TILES, (BLOCKS, BLOCKS))
    place = lax.broadcasted_iota(jnp.int32, (BLOCKS, BLOCKS), 1)
    line = lax.broadcasted_iota(jnp.int32, (BLOCKS, BLOCKS), 0)
    own_id = jnp.max(jnp.where(place == line, ids, 0), axis=1, keepdims=True)
    before = jnp.where(jnp.logical_and(ids == own_id, place < line), place + 1, 0)
    last = jnp.where(ids == line, place + 1, 0)
    for i, found in enumerate((before, last)):
        links_vector[BLOCKS * i : BLOCKS * i + BLOCKS, :] = jnp.broadcast_to(
            jnp.max(found, axis=1, keepdims=True), (BLOCKS, 128)
        )
    links_copy = pltpu.make_async_copy(links_vector, links, links_sem)
    links_copy.start()

    for load in loads[:3]:
        load.wait()
    planes[:, 1 : ROWS + 1, 0:PAD, :] = jnp.zeros((2, ROWS, PAD, NZ), jnp.float32)
    planes[:, 1 : ROWS + 1, PAD + NL :, :] = jnp.zeros((2, ROWS, PAD, NZ), jnp.float32)

    def coil_block(i, carry):
        row, part = i // 4, i % 4
        start = pl.multiple_of(part * 128, 128)
        low = low_lanes((128, 128))
        pieces = matmul(split[...], maps[row, pl.ds(pl.multiple_of(part * 256, 256), 256), :])
        pieces = pieces * (1.0 / NL)
        real, imag = pieces[:128], pieces[128:]
        real_sw, imag_sw = swap(real), swap(imag)
        field = image.at[row, pl.ds(pl.multiple_of(part * 256, 256), 256), :]
        f_real, f_imag = field[pl.ds(0, 128, 2), :], field[pl.ds(1, 128, 2), :]
        planes[0, row + 1, pl.ds(start + PAD, 128), :] = f_real
        planes[1, row + 1, pl.ds(start + PAD, 128), :] = f_imag
        f_real_sw, f_imag_sw = swap(f_real), swap(f_imag)
        by_half = (
            (jnp.where(low, real, real_sw), jnp.where(low, imag, -imag_sw), jnp.where(low, f_real, f_imag_sw), jnp.where(low, f_imag, f_real_sw)),
            (jnp.where(low, real_sw, real), jnp.where(low, imag_sw, -imag), jnp.where(low, f_real_sw, f_imag), jnp.where(low, f_imag_sw, f_real)),
        )
        for half, (m_real, m_imag, f, f_sw) in enumerate(by_half):
            map_real[half, row, pl.ds(start, 128), :] = m_real.astype(jnp.bfloat16)
            map_imag[half, row, pl.ds(start, 128), :] = m_imag.astype(jnp.bfloat16)
            value = m_real * f - m_imag * f_sw
            turned = swap(value)
            lanes = pl.ds(pl.multiple_of(row * 128, 128), 128)
            packed[half, pl.ds(start, 128), lanes] = value.astype(jnp.bfloat16)
            packed[half, pl.ds(start + NL, 128), lanes] = jnp.where(low, turned, -turned).astype(jnp.bfloat16)
        return carry

    lax.fori_loop(0, 16, coil_block, 0)
    loads[3].wait()

    def to_send(half, send):
        def step(i, carry):
            rows = pl.ds(pl.multiple_of(i * 256, 256), 256)
            send[half, pl.ds(i * 64, 64)] = to_messages(matmul(table[rows, :], packed[half]))
            return carry

        lax.fori_loop(0, 2, step, 0)

    def post(half, send, recv, send_sem, recv_sem, own_index):
        def step(d):
            pltpu.make_async_remote_copy(
                send.at[half, d],
                recv.at[half, me],
                send_sem.at[half],
                recv_sem.at[half],
                device_id=(d, coil),
                device_id_type=MESH,
            ).start()

        own = pltpu.make_async_copy(send.at[half, me], recv.at[half, me], own_sem.at[own_index])
        own.start()
        for_partners(step)
        return own

    def await_all(half, ref, sem):
        part = ref.at[half, pl.ds(0, PENS - 1)]
        pltpu.make_async_copy(part, part, sem.at[half]).wait()

    def unpack(half, recv, sign):
        def widen(i, carry):
            wide[pl.ds(pl.multiple_of(i * 256, 256), 256), :] = (
                recv[half, pl.ds(i * 16, 16)].reshape(256, 128).astype(jnp.float32)
            )
            return carry

        lax.fori_loop(0, 8, widen, 0)
        low = low_lanes((128, 128))
        for a in range(4):
            for part in range(4):
                value = wide[pl.ds(a + 512 * part, 128, 4), :]
                turned = swap(value) * sign
                lanes = slice(a * 128, a * 128 + 128)
                packed[half, 128 * part : 128 * part + 128, lanes] = value.astype(jnp.bfloat16)
                packed[half, NL + 128 * part : NL + 128 * part + 128, lanes] = jnp.where(
                    low, turned, -turned
                ).astype(jnp.bfloat16)

    to_send(0, send_fwd)
    pl.semaphore_wait(barrier, PENS)
    own0 = post(0, send_fwd, recv_fwd, fwd_send_sem, fwd_recv_sem, 0)
    to_send(1, send_fwd)
    own1 = post(1, send_fwd, recv_fwd, fwd_send_sem, fwd_recv_sem, 1)

    window = pl.ds(pl.multiple_of(coil * HALF, HALF), HALF + 2 * PAD)
    halos = []
    for i, (source, place, to) in enumerate(((1, ROWS + 1, me + PENS - 1), (ROWS, 0, me + 1))):
        halo = pltpu.make_async_remote_copy(
            planes.at[:, source, window],
            planes.at[:, place, window],
            halo_send_sem.at[i],
            halo_recv_sem.at[i],
            device_id=(to % PENS, coil),
            device_id_type=MESH,
        )
        halo.start()
        halos.append(halo)

    loads[4].wait()
    loads[5].wait()
    links_copy.wait()
    history[0] = jnp.zeros((TILE, 3 * 128), jnp.float32)

    def chain(i, carry):
        weights = kernels[i]
        pieces = matmul(split[...], samples[i]).astype(jnp.bfloat16)
        right = jnp.concatenate([weights, pieces[:128], pieces[128:]], 1)
        term = lax.dot_general(weights, right, (((0,), (0,)), ((), ())), preferred_element_type=jnp.float32)
        history[i + 1] = history[jnp.clip(links[i, 0], 0, BLOCKS)] + term
        return carry

    lax.fori_loop(0, BLOCKS, chain, 0)

    def finish(tile, carry):
        total = history[jnp.clip(links[BLOCKS + tile, 0], 0, BLOCKS)]
        low = low_lanes((128, 128))
        gram[tile] = total[:, :128].astype(jnp.bfloat16)
        real, imag = total[:, 128:256], total[:, 256:]
        target[0, tile] = jnp.where(low, real, swap(imag))
        target[1, tile] = jnp.where(low, swap(real), imag)
        return carry

    lax.fori_loop(0, TILES, finish, 0)

    def grid_side(half, own):
        await_all(half, recv_fwd, fwd_recv_sem)
        own.wait()
        unpack(half, recv_fwd, 1.0)
        low = low_lanes((128, 128))
        spectrum = []
        for i in range(2):
            spectrum.append(matmul(table[256 * i : 256 * i + 256, :], packed[half]).astype(jnp.bfloat16))
        for i in range(2):
            for k in range(2):
                quarter = 2 * i + k
                for column in range(4):
                    lanes = slice(column * 128, column * 128 + 128)
                    cells = spectrum[i][128 * k : 128 * k + 128, lanes]
                    tile = 4 * column + quarter
                    value = matmul(gram[tile], cells) - target[half, tile]
                    turned = swap(value)
                    packed[half, 128 * quarter : 128 * quarter + 128, lanes] = value.astype(jnp.bfloat16)
                    packed[half, NL + 128 * quarter : NL + 128 * quarter + 128, lanes] = jnp.where(
                        low, -turned, turned
                    ).astype(jnp.bfloat16)
        to_send(half, send_back)
        return post(half, send_back, recv_back, back_send_sem, back_recv_sem, 2 + half)

    own2 = grid_side(0, own0)

    for halo in halos:
        halo.wait_recv()
    first_col = coil * HALF

    def tv_columns(i, carry):
        lane = lax.broadcasted_iota(jnp.int32, (72, 128), 1)
        cols = lax.broadcasted_iota(jnp.int32, (72, 128), 0) + (first_col + i * 64 - PAD)
        col_ok = jnp.logical_and(cols >= 0, cols != NL - 1)
        start = pl.multiple_of(first_col + i * 64, 64)

        def tv_row(k, before):
            row = me * ROWS + k - 1
            row_ok = jnp.logical_and(row >= 0, row != NL - 1).astype(jnp.float32)
            diffs, squares = [], 1.0
            for r in range(2):
                here = planes[r, k, pl.ds(start, 80), :]
                above = planes[r, k + 1, pl.ds(start, 72), :]
                center = here[:72]
                diff_y = (above - center) * row_ok
                diff_x = jnp.where(col_ok, here[1:73] - center, 0.0)
                diff_z = jnp.where(lane == NZ - 1, 0.0, pltpu.roll(center, NZ - 1, 1) - center)
                squares = squares + (diff_y * diff_y + diff_x * diff_x + diff_z * diff_z)
                diffs.append((diff_y, diff_x, diff_z))
            inverse = TV_WEIGHT / jnp.sqrt(squares)
            after = []
            for r in range(2):
                flux_y, flux_x, flux_z = (diff * inverse for diff in diffs[r])
                flux_y, flux_z = flux_y[8:], flux_z[8:]
                shifted = jnp.where(lane[8:] == 0, 0.0, pltpu.roll(flux_z, 1, 1))
                tv_part[k, pl.ds(pl.multiple_of(i * 128, 128) + r, 64, 2), :] = (
                    before[r] - flux_y + flux_x[7:71] - flux_x[8:] + shifted - flux_z
                )
                after.append(flux_y)
            return tuple(after)

        zero = jnp.zeros((64, 128), jnp.float32)
        lax.fori_loop(0, ROWS + 1, tv_row, (zero, zero))
        return carry

    lax.fori_loop(0, HALF // 64, tv_columns, 0)
    tv_store = pltpu.make_async_copy(tv_part.at[pl.ds(1, ROWS)], tv_out, store_sem.at[ROWS])
    tv_store.start()

    own3 = grid_side(1, own1)

    def coil_terms(half, side):
        columns = pl.ds(pl.multiple_of(side * HALF, HALF), HALF)
        result = matmul(table[columns, :], packed[half])
        for row in range(ROWS):
            value = result[:, row * 128 : row * 128 + 128]
            real = map_real[half, row, columns, :].astype(jnp.float32)
            imag = map_imag[half, row, columns, :].astype(jnp.float32)
            yield row, real * value + imag * swap(value)

    def image_side(half, own):
        await_all(half, recv_back, back_recv_sem)
        own.wait()
        unpack(half, recv_back, -1.0)
        copies = []
        for row, term in coil_terms(half, other):
            send_term[half, row] = term.astype(jnp.bfloat16)
            copy = pltpu.make_async_remote_copy(
                send_term.at[half, row],
                recv_term.at[half, row],
                term_send_sem.at[half, row],
                term_recv_sem.at[half, row],
                device_id=(me, other),
                device_id_type=MESH,
            )
            copy.start()
            copies.append(copy)
        for row, term in coil_terms(half, coil):
            own_term[half, row] = term
        return copies

    first_copies = image_side(0, own2)
    second_copies = image_side(1, own3)
    for halo in halos:
        halo.wait_send()
    for half in range(2):
        await_all(half, send_fwd, fwd_send_sem)
        await_all(half, send_back, back_send_sem)
    tv_store.wait()

    stores = []
    low = low_lanes((HALF, 128))
    for row in range(ROWS):
        first_copies[row].wait()
        second_copies[row].wait()
        first = own_term[0, row] + recv_term[0, row].astype(jnp.float32)
        second = own_term[1, row] + recv_term[1, row].astype(jnp.float32)
        data_part[row, pl.ds(0, HALF, 2), :] = jnp.where(low, first, swap(second))
        data_part[row, pl.ds(1, HALF, 2), :] = jnp.where(low, swap(first), second)
        store = pltpu.make_async_copy(data_part.at[row], data_out.at[row], store_sem.at[row])
        store.start()
        stores.append(store)
    for store in stores:
        store.wait()


def on_device(image_field, coil_maps, samples, kernels, tile_of_block):
    bf16, f32 = jnp.bfloat16, jnp.float32
    dma = pltpu.SemaphoreType.DMA
    hbm = pl.BlockSpec(memory_space=pl.ANY)
    data_part, tv_part = pl.pallas_call(
        body,
        out_shape=[jax.ShapeDtypeStruct((ROWS, 2 * HALF, NZ), f32)] * 2,
        in_specs=[pl.BlockSpec(memory_space=pltpu.VMEM)] + [hbm] * 6,
        out_specs=[hbm] * 2,
        scratch_shapes=[
            pltpu.VMEM((ROWS, 2 * NL, NZ), f32),
            pltpu.VMEM((ROWS, 2 * NL, NZ), bf16),
            pltpu.VMEM((BLOCKS, 256, NZ), bf16),
            pltpu.VMEM((BLOCKS, TILE, TILE), bf16),
            pltpu.VMEM((NL, 2 * NL), bf16),
            pltpu.VMEM((256, 256), bf16),
            pltpu.VMEM((2, ROWS + 2, NL + 2 * PAD, NZ), f32),
            pltpu.VMEM((2, ROWS, NL, NZ), bf16),
            pltpu.VMEM((2, ROWS, NL, NZ), bf16),
            pltpu.VMEM((2, 2 * NL, 4 * 128), bf16),
            pltpu.VMEM((2, PENS, 16, 128), bf16),
            pltpu.VMEM((2, PENS, 16, 128), bf16),
            pltpu.VMEM((2, PENS, 16, 128), bf16),
            pltpu.VMEM((2, PENS, 16, 128), bf16),
            pltpu.VMEM((BLOCKS + 1, TILE, 3 * 128), f32),
            pltpu.VMEM((TILES, TILE, TILE), bf16),
            pltpu.VMEM((2, TILES, TILE, 128), f32),
            pltpu.VMEM((PENS * 16, 128), f32),
            pltpu.VMEM((2, ROWS, HALF, 128), f32),
            pltpu.VMEM((2, ROWS, HALF, 128), bf16),
            pltpu.VMEM((2, ROWS, HALF, 128), bf16),
            pltpu.VMEM((ROWS + 1, 2 * HALF, 128), f32),
            pltpu.VMEM((ROWS, 2 * HALF, 128), f32),
            pltpu.VMEM((2 * BLOCKS, 128), jnp.int32),
            pltpu.SMEM((2 * BLOCKS, 128), jnp.int32),
            dma((6,)),
            dma((4,)),
            dma((2,)),
            dma((2,)),
            dma((2,)),
            dma((2,)),
            dma((2, ROWS)),
            dma((2, ROWS)),
            dma((ROWS + 1,)),
            dma((2,)),
            dma((2,)),
            dma(()),
        ],
        compiler_params=pltpu.CompilerParams(
            collective_id=0, has_side_effects=True, vmem_limit_bytes=56 << 20
        ),
        name="adjoint_gradient",
    )(
        tile_of_block.reshape(1, BLOCKS),
        image_field.reshape(ROWS, 2 * NL, NZ),
        coil_maps.reshape(ROWS, 2 * NL, NZ),
        samples.reshape(BLOCKS, 256, NZ),
        kernels,
        jnp.asarray(dft_table()),
        jnp.asarray(split_table()),
    )
    return (data_part + tv_part).reshape(ROWS, HALF, 2, NZ)


def solution(mesh):
    in_specs = (
        P("pen", None, None, None),
        P("coil", "pen", None, None, None),
        P("coil", "pen", None, None, None),
        P("pen", None, None),
        P("pen"),
    )
    out_specs = P("pen", "coil", None, None)
    return jax.shard_map(
        on_device, mesh=mesh, in_specs=in_specs, out_specs=out_specs, check_vma=False
    )
```

```python
import numpy as np

import jax
import jax.numpy as jnp
from jax import lax
from jax.experimental import pallas as pl
from jax.experimental.pallas import tpu as pltpu
from jax.sharding import PartitionSpec as P

NL = 512
NZ = 128
TILE = 128
PENS = 128
ROWS = 4
BLOCKS = 32
TILES = 16
HALF = NL // 2
PAD = 8
TV_WEIGHT = 2.0
MESH = pl.DeviceIdType.MESH


def dft_table():
    index = np.arange(NL)
    angle = 2.0 * np.pi / NL * (index[:, None] * index[None, :] % NL)
    return np.concatenate([np.cos(angle), np.sin(angle)], 1).astype(jnp.bfloat16)


def split_table():
    table = np.zeros((256, 256), np.float32)
    index = np.arange(128)
    table[index, 2 * index] = 1.0
    table[128 + index, 2 * index + 1] = 1.0
    return table.astype(jnp.bfloat16)


def low_lanes(shape):
    return lax.broadcasted_iota(jnp.int32, shape, len(shape) - 1) < 64


def swap(value):
    return pltpu.roll(value, 64, 1)


def matmul(left, right):
    return jnp.dot(left, right, preferred_element_type=jnp.float32)


def to_messages(result):
    count = result.shape[0] // 8
    groups = [result[:, 128 * a : 128 * (a + 1)].reshape(count, 8, 128) for a in range(4)]
    upper = lax.broadcasted_iota(jnp.int32, (count, 8, 128), 1) < 4
    even, odd = [], []
    for a in (0, 2):
        first, second = groups[a], groups[a + 1]
        even.append(jnp.where(upper, first, pltpu.roll(second, 4, 1)))
        odd.append(jnp.where(upper, pltpu.roll(first, 4, 1), second))
    both = jnp.stack([jnp.concatenate(even, 1), jnp.concatenate(odd, 1)], 1)
    return both.reshape(2 * count, 16, 128).astype(jnp.bfloat16)


def body(
    tile_ids,
    image_hbm,
    maps_hbm,
    samples_hbm,
    kernels_hbm,
    table_hbm,
    split_hbm,
    data_out,
    tv_out,
    image,
    maps,
    samples,
    kernels,
    table,
    split,
    planes,
    map_real,
    map_imag,
    packed,
    send_fwd,
    recv_fwd,
    send_back,
    recv_back,
    history,
    gram,
    target,
    wide,
    own_term,
    send_term,
    recv_term,
    tv_part,
    data_part,
    halo_out,
    halo_in,
    links_vector,
    links,
    load_sem,
    own_sem,
    fwd_send_sem,
    fwd_recv_sem,
    back_send_sem,
    back_recv_sem,
    term_send_sem,
    term_recv_sem,
    store_sem,
    halo_send_sem,
    halo_recv_sem,
    links_sem,
):
    me = lax.axis_index("pen")
    coil = lax.axis_index("coil")
    other = 1 - coil
    y, z, rest = me // 64, me // 8 % 8, me % 8
    ring = [(z + d) % 8 * 8 for d in (4, 3, 5, 2, 6, 1, 7, 0)]

    def for_partners(act):
        def group(i, carry):
            base = (y + 1 - i // 8) % 2 * 64 + (rest + 15 - i) % 8
            for place in ring:
                act(base + place)
            return carry

        lax.fori_loop(0, 15, group, 0)
        for place in ring[:7]:
            act(y * 64 + rest + place)

    pairs = (
        (image_hbm, image),
        (maps_hbm, maps),
        (split_hbm, split),
        (table_hbm, table),
        (kernels_hbm, kernels),
        (samples_hbm, samples),
    )
    loads = [pltpu.make_async_copy(a, b, load_sem.at[i]) for i, (a, b) in enumerate(pairs)]
    for load in loads:
        load.start()

    barrier = pltpu.get_barrier_semaphore()

    def greet(d):
        pl.semaphore_signal(barrier, inc=1, device_id=(d, coil), device_id_type=MESH)

    for_partners(greet)
    pl.semaphore_signal(barrier, inc=1, device_id=(me, other), device_id_type=MESH)

    ids = jnp.broadcast_to(tile_ids[...] % TILES, (BLOCKS, BLOCKS))
    place = lax.broadcasted_iota(jnp.int32, (BLOCKS, BLOCKS), 1)
    line = lax.broadcasted_iota(jnp.int32, (BLOCKS, BLOCKS), 0)
    own_id = jnp.max(jnp.where(place == line, ids, 0), axis=1, keepdims=True)
    before = jnp.where(jnp.logical_and(ids == own_id, place < line), place + 1, 0)
    last = jnp.where(ids == line, place + 1, 0)
    for i, found in enumerate((before, last)):
        links_vector[BLOCKS * i : BLOCKS * i + BLOCKS, :] = jnp.broadcast_to(
            jnp.max(found, axis=1, keepdims=True), (BLOCKS, 128)
        )
    links_copy = pltpu.make_async_copy(links_vector, links, links_sem)
    links_copy.start()

    for load in loads[:3]:
        load.wait()
    planes[:, 1 : ROWS + 1, 0:PAD, :] = jnp.zeros((2, ROWS, PAD, NZ), jnp.float32)
    planes[:, 1 : ROWS + 1, PAD + NL :, :] = jnp.zeros((2, ROWS, PAD, NZ), jnp.float32)

    def coil_block(i, carry):
        row, part = i // 4, i % 4
        start = pl.multiple_of(part * 128, 128)
        low = low_lanes((128, 128))
        pieces = matmul(split[...], maps[row, pl.ds(pl.multiple_of(part * 256, 256), 256), :])
        pieces = pieces * (1.0 / NL)
        real, imag = pieces[:128], pieces[128:]
        real_sw, imag_sw = swap(real), swap(imag)
        field = image.at[row, pl.ds(pl.multiple_of(part * 256, 256), 256), :]
        f_real, f_imag = field[pl.ds(0, 128, 2), :], field[pl.ds(1, 128, 2), :]
        planes[0, row + 1, pl.ds(start + PAD, 128), :] = f_real
        planes[1, row + 1, pl.ds(start + PAD, 128), :] = f_imag
        f_real_sw, f_imag_sw = swap(f_real), swap(f_imag)
        by_half = (
            (jnp.where(low, real, real_sw), jnp.where(low, imag, -imag_sw), jnp.where(low, f_real, f_imag_sw), jnp.where(low, f_imag, f_real_sw)),
            (jnp.where(low, real_sw, real), jnp.where(low, imag_sw, -imag), jnp.where(low, f_real_sw, f_imag), jnp.where(low, f_imag_sw, f_real)),
        )
        for half, (m_real, m_imag, f, f_sw) in enumerate(by_half):
            map_real[half, row, pl.ds(start, 128), :] = m_real.astype(jnp.bfloat16)
            map_imag[half, row, pl.ds(start, 128), :] = m_imag.astype(jnp.bfloat16)
            value = m_real * f - m_imag * f_sw
            turned = swap(value)
            lanes = pl.ds(pl.multiple_of(row * 128, 128), 128)
            packed[half, pl.ds(start, 128), lanes] = value.astype(jnp.bfloat16)
            packed[half, pl.ds(start + NL, 128), lanes] = jnp.where(low, turned, -turned).astype(jnp.bfloat16)
        return carry

    lax.fori_loop(0, 16, coil_block, 0)
    loads[3].wait()

    def to_send(half, send):
        def step(i, carry):
            rows = pl.ds(pl.multiple_of(i * 256, 256), 256)
            send[half, pl.ds(i * 64, 64)] = to_messages(matmul(table[rows, :], packed[half]))
            return carry

        lax.fori_loop(0, 2, step, 0)

    def post(half, send, recv, send_sem, recv_sem, own_index):
        def step(d):
            pltpu.make_async_remote_copy(
                send.at[half, d],
                recv.at[half, me],
                send_sem.at[half],
                recv_sem.at[half],
                device_id=(d, coil),
                device_id_type=MESH,
            ).start()

        own = pltpu.make_async_copy(send.at[half, me], recv.at[half, me], own_sem.at[own_index])
        own.start()
        for_partners(step)
        return own

    def await_all(half, ref, sem):
        part = ref.at[half, pl.ds(0, PENS - 1)]
        pltpu.make_async_copy(part, part, sem.at[half]).wait()

    def unpack(half, recv, sign):
        def widen(i, carry):
            wide[pl.ds(pl.multiple_of(i * 256, 256), 256), :] = (
                recv[half, pl.ds(i * 16, 16)].reshape(256, 128).astype(jnp.float32)
            )
            return carry

        lax.fori_loop(0, 8, widen, 0)
        low = low_lanes((128, 128))
        for a in range(4):
            for part in range(4):
                value = wide[pl.ds(a + 512 * part, 128, 4), :]
                turned = swap(value) * sign
                lanes = slice(a * 128, a * 128 + 128)
                packed[half, 128 * part : 128 * part + 128, lanes] = value.astype(jnp.bfloat16)
                packed[half, NL + 128 * part : NL + 128 * part + 128, lanes] = jnp.where(
                    low, turned, -turned
                ).astype(jnp.bfloat16)

    to_send(0, send_fwd)
    pl.semaphore_wait(barrier, PENS)
    own0 = post(0, send_fwd, recv_fwd, fwd_send_sem, fwd_recv_sem, 0)
    to_send(1, send_fwd)
    own1 = post(1, send_fwd, recv_fwd, fwd_send_sem, fwd_recv_sem, 1)

    window = pl.ds(pl.multiple_of(coil * HALF, HALF), HALF + 2 * PAD)
    halos = []
    for i, (source, to) in enumerate(((1, me + PENS - 1), (ROWS, me + 1))):
        halo_out[i] = planes[:, source, window, :].astype(jnp.bfloat16)
        halo = pltpu.make_async_remote_copy(
            halo_out.at[i],
            halo_in.at[i],
            halo_send_sem.at[i],
            halo_recv_sem.at[i],
            device_id=(to % PENS, coil),
            device_id_type=MESH,
        )
        halo.start()
        halos.append(halo)

    loads[4].wait()
    loads[5].wait()
    links_copy.wait()
    history[0] = jnp.zeros((TILE, 3 * 128), jnp.float32)

    def chain(i, carry):
        weights = kernels[i]
        pieces = matmul(split[...], samples[i]).astype(jnp.bfloat16)
        right = jnp.concatenate([weights, pieces[:128], pieces[128:]], 1)
        term = lax.dot_general(weights, right, (((0,), (0,)), ((), ())), preferred_element_type=jnp.float32)
        history[i + 1] = history[jnp.clip(links[i, 0], 0, BLOCKS)] + term
        return carry

    lax.fori_loop(0, BLOCKS, chain, 0)

    def finish(tile, carry):
        total = history[jnp.clip(links[BLOCKS + tile, 0], 0, BLOCKS)]
        low = low_lanes((128, 128))
        gram[tile] = total[:, :128].astype(jnp.bfloat16)
        real, imag = total[:, 128:256], total[:, 256:]
        target[0, tile] = jnp.where(low, real, swap(imag))
        target[1, tile] = jnp.where(low, swap(real), imag)
        return carry

    lax.fori_loop(0, TILES, finish, 0)

    def grid_side(half, own):
        await_all(half, recv_fwd, fwd_recv_sem)
        own.wait()
        unpack(half, recv_fwd, 1.0)
        low = low_lanes((128, 128))
        spectrum = []
        for i in range(2):
            spectrum.append(matmul(table[256 * i : 256 * i + 256, :], packed[half]).astype(jnp.bfloat16))
        for i in range(2):
            for k in range(2):
                quarter = 2 * i + k
                for column in range(4):
                    lanes = slice(column * 128, column * 128 + 128)
                    cells = spectrum[i][128 * k : 128 * k + 128, lanes]
                    tile = 4 * column + quarter
                    value = matmul(gram[tile], cells) - target[half, tile]
                    turned = swap(value)
                    packed[half, 128 * quarter : 128 * quarter + 128, lanes] = value.astype(jnp.bfloat16)
                    packed[half, NL + 128 * quarter : NL + 128 * quarter + 128, lanes] = jnp.where(
                        low, -turned, turned
                    ).astype(jnp.bfloat16)
        to_send(half, send_back)
        return post(half, send_back, recv_back, back_send_sem, back_recv_sem, 2 + half)

    own2 = grid_side(0, own0)

    own3 = grid_side(1, own1)

    for i, place in enumerate((ROWS + 1, 0)):
        halos[i].wait_recv()
        planes[:, place, window, :] = halo_in[i].astype(jnp.float32)
    first_col = coil * HALF

    def tv_columns(i, carry):
        lane = lax.broadcasted_iota(jnp.int32, (72, 128), 1)
        cols = lax.broadcasted_iota(jnp.int32, (72, 128), 0) + (first_col + i * 64 - PAD)
        col_ok = jnp.logical_and(cols >= 0, cols != NL - 1)
        start = pl.multiple_of(first_col + i * 64, 64)

        def tv_row(k, before):
            row = me * ROWS + k - 1
            row_ok = jnp.logical_and(row >= 0, row != NL - 1).astype(jnp.float32)
            diffs, squares = [], 1.0
            for r in range(2):
                here = planes[r, k, pl.ds(start, 80), :]
                above = planes[r, k + 1, pl.ds(start, 72), :]
                center = here[:72]
                diff_y = (above - center) * row_ok
                diff_x = jnp.where(col_ok, here[1:73] - center, 0.0)
                diff_z = jnp.where(lane == NZ - 1, 0.0, pltpu.roll(center, NZ - 1, 1) - center)
                squares = squares + (diff_y * diff_y + diff_x * diff_x + diff_z * diff_z)
                diffs.append((diff_y, diff_x, diff_z))
            inverse = TV_WEIGHT / jnp.sqrt(squares)
            after = []
            for r in range(2):
                flux_y, flux_x, flux_z = (diff * inverse for diff in diffs[r])
                flux_y, flux_z = flux_y[8:], flux_z[8:]
                shifted = jnp.where(lane[8:] == 0, 0.0, pltpu.roll(flux_z, 1, 1))
                tv_part[k, pl.ds(pl.multiple_of(i * 128, 128) + r, 64, 2), :] = (
                    before[r] - flux_y + flux_x[7:71] - flux_x[8:] + shifted - flux_z
                )
                after.append(flux_y)
            return tuple(after)

        zero = jnp.zeros((64, 128), jnp.float32)
        lax.fori_loop(0, ROWS + 1, tv_row, (zero, zero))
        return carry

    lax.fori_loop(0, HALF // 64, tv_columns, 0)
    tv_store = pltpu.make_async_copy(tv_part.at[pl.ds(1, ROWS)], tv_out, store_sem.at[ROWS])
    tv_store.start()

    def coil_terms(half, side):
        columns = pl.ds(pl.multiple_of(side * HALF, HALF), HALF)
        result = matmul(table[columns, :], packed[half])
        for row in range(ROWS):
            value = result[:, row * 128 : row * 128 + 128]
            real = map_real[half, row, columns, :].astype(jnp.float32)
            imag = map_imag[half, row, columns, :].astype(jnp.float32)
            yield row, real * value + imag * swap(value)

    def image_side(half, own):
        await_all(half, recv_back, back_recv_sem)
        own.wait()
        unpack(half, recv_back, -1.0)
        copies = []
        for row, term in coil_terms(half, other):
            send_term[half, row] = term.astype(jnp.bfloat16)
            copy = pltpu.make_async_remote_copy(
                send_term.at[half, row],
                recv_term.at[half, row],
                term_send_sem.at[half, row],
                term_recv_sem.at[half, row],
                device_id=(me, other),
                device_id_type=MESH,
            )
            copy.start()
            copies.append(copy)
        for row, term in coil_terms(half, coil):
            own_term[half, row] = term
        return copies

    first_copies = image_side(0, own2)
    second_copies = image_side(1, own3)
    for halo in halos:
        halo.wait_send()
    for half in range(2):
        await_all(half, send_fwd, fwd_send_sem)
        await_all(half, send_back, back_send_sem)
    tv_store.wait()

    stores = []
    low = low_lanes((HALF, 128))
    for row in range(ROWS):
        first_copies[row].wait()
        second_copies[row].wait()
        first = own_term[0, row] + recv_term[0, row].astype(jnp.float32)
        second = own_term[1, row] + recv_term[1, row].astype(jnp.float32)
        data_part[row, pl.ds(0, HALF, 2), :] = jnp.where(low, first, swap(second))
        data_part[row, pl.ds(1, HALF, 2), :] = jnp.where(low, swap(first), second)
        store = pltpu.make_async_copy(data_part.at[row], data_out.at[row], store_sem.at[row])
        store.start()
        stores.append(store)
    for store in stores:
        store.wait()


def on_device(image_field, coil_maps, samples, kernels, tile_of_block):
    bf16, f32 = jnp.bfloat16, jnp.float32
    dma = pltpu.SemaphoreType.DMA
    hbm = pl.BlockSpec(memory_space=pl.ANY)
    data_part, tv_part = pl.pallas_call(
        body,
        out_shape=[jax.ShapeDtypeStruct((ROWS, 2 * HALF, NZ), f32)] * 2,
        in_specs=[pl.BlockSpec(memory_space=pltpu.VMEM)] + [hbm] * 6,
        out_specs=[hbm] * 2,
        scratch_shapes=[
            pltpu.VMEM((ROWS, 2 * NL, NZ), f32),
            pltpu.VMEM((ROWS, 2 * NL, NZ), bf16),
            pltpu.VMEM((BLOCKS, 256, NZ), bf16),
            pltpu.VMEM((BLOCKS, TILE, TILE), bf16),
            pltpu.VMEM((NL, 2 * NL), bf16),
            pltpu.VMEM((256, 256), bf16),
            pltpu.VMEM((2, ROWS + 2, NL + 2 * PAD, NZ), f32),
            pltpu.VMEM((2, ROWS, NL, NZ), bf16),
            pltpu.VMEM((2, ROWS, NL, NZ), bf16),
            pltpu.VMEM((2, 2 * NL, 4 * 128), bf16),
            pltpu.VMEM((2, PENS, 16, 128), bf16),
            pltpu.VMEM((2, PENS, 16, 128), bf16),
            pltpu.VMEM((2, PENS, 16, 128), bf16),
            pltpu.VMEM((2, PENS, 16, 128), bf16),
            pltpu.VMEM((BLOCKS + 1, TILE, 3 * 128), f32),
            pltpu.VMEM((TILES, TILE, TILE), bf16),
            pltpu.VMEM((2, TILES, TILE, 128), f32),
            pltpu.VMEM((PENS * 16, 128), f32),
            pltpu.VMEM((2, ROWS, HALF, 128), f32),
            pltpu.VMEM((2, ROWS, HALF, 128), bf16),
            pltpu.VMEM((2, ROWS, HALF, 128), bf16),
            pltpu.VMEM((ROWS + 1, 2 * HALF, 128), f32),
            pltpu.VMEM((ROWS, 2 * HALF, 128), f32),
            pltpu.VMEM((2, 2, HALF + 2 * PAD, 128), bf16),
            pltpu.VMEM((2, 2, HALF + 2 * PAD, 128), bf16),
            pltpu.VMEM((2 * BLOCKS, 128), jnp.int32),
            pltpu.SMEM((2 * BLOCKS, 128), jnp.int32),
            dma((6,)),
            dma((4,)),
            dma((2,)),
            dma((2,)),
            dma((2,)),
            dma((2,)),
            dma((2, ROWS)),
            dma((2, ROWS)),
            dma((ROWS + 1,)),
            dma((2,)),
            dma((2,)),
            dma(()),
        ],
        compiler_params=pltpu.CompilerParams(
            collective_id=0, has_side_effects=True, vmem_limit_bytes=56 << 20
        ),
        name="adjoint_gradient",
    )(
        tile_of_block.reshape(1, BLOCKS),
        image_field.reshape(ROWS, 2 * NL, NZ),
        coil_maps.reshape(ROWS, 2 * NL, NZ),
        samples.reshape(BLOCKS, 256, NZ),
        kernels,
        jnp.asarray(dft_table()),
        jnp.asarray(split_table()),
    )
    return (data_part + tv_part).reshape(ROWS, HALF, 2, NZ)


def solution(mesh):
    in_specs = (
        P("pen", None, None, None),
        P("coil", "pen", None, None, None),
        P("coil", "pen", None, None, None),
        P("pen", None, None),
        P("pen"),
    )
    out_specs = P("pen", "coil", None, None)
    return jax.shard_map(
        on_device, mesh=mesh, in_specs=in_specs, out_specs=out_specs, check_vma=False
    )
```

```python
import numpy as np

import jax
import jax.numpy as jnp
from jax import lax
from jax.experimental import pallas as pl
from jax.experimental.pallas import tpu as pltpu
from jax.sharding import PartitionSpec as P

NL = 512
NZ = 128
TILE = 128
PENS = 128
ROWS = 4
BLOCKS = 32
TILES = 16
HALF = NL // 2
PAD = 8
TV_WEIGHT = 2.0
MESH = pl.DeviceIdType.MESH


def dft_table():
    index = np.arange(NL)
    angle = 2.0 * np.pi / NL * (index[:, None] * index[None, :] % NL)
    return np.concatenate([np.cos(angle), np.sin(angle)], 1).astype(jnp.bfloat16)


def split_table():
    table = np.zeros((256, 256), np.float32)
    index = np.arange(128)
    table[index, 2 * index] = 1.0
    table[128 + index, 2 * index + 1] = 1.0
    return table.astype(jnp.bfloat16)


def low_lanes(shape):
    return lax.broadcasted_iota(jnp.int32, shape, len(shape) - 1) < 64


def swap(value):
    return pltpu.roll(value, 64, 1)


def matmul(left, right):
    return jnp.dot(left, right, preferred_element_type=jnp.float32)


def to_messages(result):
    count = result.shape[0] // 8
    groups = [result[:, 128 * a : 128 * (a + 1)].reshape(count, 8, 128) for a in range(4)]
    upper = lax.broadcasted_iota(jnp.int32, (count, 8, 128), 1) < 4
    even, odd = [], []
    for a in (0, 2):
        first, second = groups[a], groups[a + 1]
        even.append(jnp.where(upper, first, pltpu.roll(second, 4, 1)))
        odd.append(jnp.where(upper, pltpu.roll(first, 4, 1), second))
    both = jnp.stack([jnp.concatenate(even, 1), jnp.concatenate(odd, 1)], 1)
    return both.reshape(2 * count, 16, 128).astype(jnp.bfloat16)


def body(
    tile_ids,
    image_hbm,
    maps_hbm,
    samples_hbm,
    kernels_hbm,
    table_hbm,
    split_hbm,
    data_out,
    tv_out,
    image,
    maps,
    samples,
    kernels,
    table,
    split,
    planes,
    map_real,
    map_imag,
    packed,
    send_fwd,
    recv_fwd,
    send_back,
    recv_back,
    history,
    gram,
    target,
    wide,
    own_term,
    send_term,
    recv_term,
    tv_part,
    data_part,
    halo_out,
    halo_in,
    links_vector,
    links,
    load_sem,
    own_sem,
    fwd_send_sem,
    fwd_recv_sem,
    back_send_sem,
    back_recv_sem,
    term_send_sem,
    term_recv_sem,
    store_sem,
    halo_send_sem,
    halo_recv_sem,
    links_sem,
):
    me = lax.axis_index("pen")
    coil = lax.axis_index("coil")
    other = 1 - coil
    y, z, rest = me // 64, me // 8 % 8, me % 8
    ring = [(z + d) % 8 * 8 for d in (4, 3, 5, 2, 6, 1, 7, 0)]

    def for_partners(act):
        def group(i, carry):
            base = (y + 1 - i // 8) % 2 * 64 + (rest + 15 - i) % 8
            for place in ring:
                act(base + place)
            return carry

        lax.fori_loop(0, 15, group, 0)
        for place in ring[:7]:
            act(y * 64 + rest + place)

    pairs = (
        (image_hbm, image),
        (maps_hbm, maps),
        (split_hbm, split),
        (table_hbm, table),
        (kernels_hbm, kernels),
        (samples_hbm, samples),
    )
    loads = [pltpu.make_async_copy(a, b, load_sem.at[i]) for i, (a, b) in enumerate(pairs)]
    for load in loads:
        load.start()

    barrier = pltpu.get_barrier_semaphore()

    def greet(d):
        pl.semaphore_signal(barrier, inc=1, device_id=(d, coil), device_id_type=MESH)

    for_partners(greet)
    pl.semaphore_signal(barrier, inc=1, device_id=(me, other), device_id_type=MESH)

    ids = jnp.broadcast_to(tile_ids[...] % TILES, (BLOCKS, BLOCKS))
    place = lax.broadcasted_iota(jnp.int32, (BLOCKS, BLOCKS), 1)
    line = lax.broadcasted_iota(jnp.int32, (BLOCKS, BLOCKS), 0)
    own_id = jnp.max(jnp.where(place == line, ids, 0), axis=1, keepdims=True)
    before = jnp.where(jnp.logical_and(ids == own_id, place < line), place + 1, 0)
    last = jnp.where(ids == line, place + 1, 0)
    for i, found in enumerate((before, last)):
        links_vector[BLOCKS * i : BLOCKS * i + BLOCKS, :] = jnp.broadcast_to(
            jnp.max(found, axis=1, keepdims=True), (BLOCKS, 128)
        )
    links_copy = pltpu.make_async_copy(links_vector, links, links_sem)
    links_copy.start()

    for load in loads[:3]:
        load.wait()
    planes[:, 1 : ROWS + 1, 0:PAD, :] = jnp.zeros((2, ROWS, PAD, NZ), jnp.float32)
    planes[:, 1 : ROWS + 1, PAD + NL :, :] = jnp.zeros((2, ROWS, PAD, NZ), jnp.float32)

    def coil_block(i, carry):
        row, part = i // 4, i % 4
        start = pl.multiple_of(part * 128, 128)
        low = low_lanes((128, 128))
        pieces = matmul(split[...], maps[row, pl.ds(pl.multiple_of(part * 256, 256), 256), :])
        pieces = pieces * (1.0 / NL)
        real, imag = pieces[:128], pieces[128:]
        real_sw, imag_sw = swap(real), swap(imag)
        field = image.at[row, pl.ds(pl.multiple_of(part * 256, 256), 256), :]
        f_real, f_imag = field[pl.ds(0, 128, 2), :], field[pl.ds(1, 128, 2), :]
        planes[0, row + 1, pl.ds(start + PAD, 128), :] = f_real
        planes[1, row + 1, pl.ds(start + PAD, 128), :] = f_imag
        f_real_sw, f_imag_sw = swap(f_real), swap(f_imag)
        by_half = (
            (jnp.where(low, real, real_sw), jnp.where(low, imag, -imag_sw), jnp.where(low, f_real, f_imag_sw), jnp.where(low, f_imag, f_real_sw)),
            (jnp.where(low, real_sw, real), jnp.where(low, imag_sw, -imag), jnp.where(low, f_real_sw, f_imag), jnp.where(low, f_imag_sw, f_real)),
        )
        for half, (m_real, m_imag, f, f_sw) in enumerate(by_half):
            map_real[half, row, pl.ds(start, 128), :] = m_real.astype(jnp.bfloat16)
            map_imag[half, row, pl.ds(start, 128), :] = m_imag.astype(jnp.bfloat16)
            value = m_real * f - m_imag * f_sw
            turned = swap(value)
            lanes = pl.ds(pl.multiple_of(row * 128, 128), 128)
            packed[half, pl.ds(start, 128), lanes] = value.astype(jnp.bfloat16)
            packed[half, pl.ds(start + NL, 128), lanes] = jnp.where(low, turned, -turned).astype(jnp.bfloat16)
        return carry

    lax.fori_loop(0, 16, coil_block, 0)
    loads[3].wait()

    def to_send(half, send):
        def step(i, carry):
            rows = pl.ds(pl.multiple_of(i * 256, 256), 256)
            send[half, pl.ds(i * 64, 64)] = to_messages(matmul(table[rows, :], packed[half]))
            return carry

        lax.fori_loop(0, 2, step, 0)

    def post(half, send, recv, send_sem, recv_sem, own_index):
        def step(d):
            pltpu.make_async_remote_copy(
                send.at[half, d],
                recv.at[half, me],
                send_sem.at[half],
                recv_sem.at[half],
                device_id=(d, coil),
                device_id_type=MESH,
            ).start()

        own = pltpu.make_async_copy(send.at[half, me], recv.at[half, me], own_sem.at[own_index])
        own.start()
        for_partners(step)
        return own

    def await_all(half, ref, sem):
        part = ref.at[half, pl.ds(0, PENS - 1)]
        pltpu.make_async_copy(part, part, sem.at[half]).wait()

    def unpack(half, recv, sign, groups=range(4), load=True):
        def widen(i, carry):
            wide[pl.ds(pl.multiple_of(i * 256, 256), 256), :] = (
                recv[half, pl.ds(i * 16, 16)].reshape(256, 128).astype(jnp.float32)
            )
            return carry

        if load:
            lax.fori_loop(0, 8, widen, 0)
        low = low_lanes((128, 128))
        for a in groups:
            for part in range(4):
                value = wide[pl.ds(a + 512 * part, 128, 4), :]
                turned = swap(value) * sign
                lanes = slice(a * 128, a * 128 + 128)
                packed[half, 128 * part : 128 * part + 128, lanes] = value.astype(jnp.bfloat16)
                packed[half, NL + 128 * part : NL + 128 * part + 128, lanes] = jnp.where(
                    low, turned, -turned
                ).astype(jnp.bfloat16)

    to_send(0, send_fwd)
    pl.semaphore_wait(barrier, PENS)
    own0 = post(0, send_fwd, recv_fwd, fwd_send_sem, fwd_recv_sem, 0)
    to_send(1, send_fwd)
    own1 = post(1, send_fwd, recv_fwd, fwd_send_sem, fwd_recv_sem, 1)

    window = pl.ds(pl.multiple_of(coil * HALF, HALF), HALF + 2 * PAD)
    halos = []
    for i, (source, to) in enumerate(((1, me + PENS - 1), (ROWS, me + 1))):
        halo_out[i] = planes[:, source, window, :].astype(jnp.bfloat16)
        halo = pltpu.make_async_remote_copy(
            halo_out.at[i],
            halo_in.at[i],
            halo_send_sem.at[i],
            halo_recv_sem.at[i],
            device_id=(to % PENS, coil),
            device_id_type=MESH,
        )
        halo.start()
        halos.append(halo)

    loads[4].wait()
    loads[5].wait()
    links_copy.wait()
    history[0] = jnp.zeros((TILE, 3 * 128), jnp.float32)

    def chain(i, carry):
        weights = kernels[i]
        pieces = matmul(split[...], samples[i]).astype(jnp.bfloat16)
        right = jnp.concatenate([weights, pieces[:128], pieces[128:]], 1)
        term = lax.dot_general(weights, right, (((0,), (0,)), ((), ())), preferred_element_type=jnp.float32)
        history[i + 1] = history[jnp.clip(links[i, 0], 0, BLOCKS)] + term
        return carry

    lax.fori_loop(0, BLOCKS, chain, 0)

    def finish(tile, carry):
        total = history[jnp.clip(links[BLOCKS + tile, 0], 0, BLOCKS)]
        low = low_lanes((128, 128))
        gram[tile] = total[:, :128].astype(jnp.bfloat16)
        real, imag = total[:, 128:256], total[:, 256:]
        target[0, tile] = jnp.where(low, real, swap(imag))
        target[1, tile] = jnp.where(low, swap(real), imag)
        return carry

    lax.fori_loop(0, TILES, finish, 0)

    def grid_side(half, own):
        await_all(half, recv_fwd, fwd_recv_sem)
        own.wait()
        unpack(half, recv_fwd, 1.0)
        low = low_lanes((128, 128))
        spectrum = []
        for i in range(2):
            spectrum.append(matmul(table[256 * i : 256 * i + 256, :], packed[half]).astype(jnp.bfloat16))
        for i in range(2):
            for k in range(2):
                quarter = 2 * i + k
                for column in range(4):
                    lanes = slice(column * 128, column * 128 + 128)
                    cells = spectrum[i][128 * k : 128 * k + 128, lanes]
                    tile = 4 * column + quarter
                    value = matmul(gram[tile], cells) - target[half, tile]
                    turned = swap(value)
                    packed[half, 128 * quarter : 128 * quarter + 128, lanes] = value.astype(jnp.bfloat16)
                    packed[half, NL + 128 * quarter : NL + 128 * quarter + 128, lanes] = jnp.where(
                        low, -turned, turned
                    ).astype(jnp.bfloat16)
        to_send(half, send_back)
        return post(half, send_back, recv_back, back_send_sem, back_recv_sem, 2 + half)

    own2 = grid_side(0, own0)

    own3 = grid_side(1, own1)

    for i, place in enumerate((ROWS + 1, 0)):
        halos[i].wait_recv()
        planes[:, place, window, :] = halo_in[i].astype(jnp.float32)
    first_col = coil * HALF

    def tv_columns(i, carry):
        lane = lax.broadcasted_iota(jnp.int32, (72, 128), 1)
        cols = lax.broadcasted_iota(jnp.int32, (72, 128), 0) + (first_col + i * 64 - PAD)
        col_ok = jnp.logical_and(cols >= 0, cols != NL - 1)
        start = pl.multiple_of(first_col + i * 64, 64)

        def tv_row(k, before):
            row = me * ROWS + k - 1
            row_ok = jnp.logical_and(row >= 0, row != NL - 1).astype(jnp.float32)
            diffs, squares = [], 1.0
            for r in range(2):
                here = planes[r, k, pl.ds(start, 80), :]
                above = planes[r, k + 1, pl.ds(start, 72), :]
                center = here[:72]
                diff_y = (above - center) * row_ok
                diff_x = jnp.where(col_ok, here[1:73] - center, 0.0)
                diff_z = jnp.where(lane == NZ - 1, 0.0, pltpu.roll(center, NZ - 1, 1) - center)
                squares = squares + (diff_y * diff_y + diff_x * diff_x + diff_z * diff_z)
                diffs.append((diff_y, diff_x, diff_z))
            inverse = TV_WEIGHT / jnp.sqrt(squares)
            after = []
            for r in range(2):
                flux_y, flux_x, flux_z = (diff * inverse for diff in diffs[r])
                flux_y, flux_z = flux_y[8:], flux_z[8:]
                shifted = jnp.where(lane[8:] == 0, 0.0, pltpu.roll(flux_z, 1, 1))
                tv_part[k, pl.ds(pl.multiple_of(i * 128, 128) + r, 64, 2), :] = (
                    before[r] - flux_y + flux_x[7:71] - flux_x[8:] + shifted - flux_z
                )
                after.append(flux_y)
            return tuple(after)

        zero = jnp.zeros((64, 128), jnp.float32)
        lax.fori_loop(0, ROWS + 1, tv_row, (zero, zero))
        return carry

    lax.fori_loop(0, HALF // 64, tv_columns, 0)
    tv_store = pltpu.make_async_copy(tv_part.at[pl.ds(1, ROWS)], tv_out, store_sem.at[ROWS])
    tv_store.start()

    def coil_terms(half, side, pair):
        columns = pl.ds(pl.multiple_of(side * HALF, HALF), HALF)
        result = matmul(table[columns, :], packed[half, :, 256 * pair : 256 * pair + 256])
        for i in range(2):
            row = 2 * pair + i
            value = result[:, i * 128 : i * 128 + 128]
            real = map_real[half, row, columns, :].astype(jnp.float32)
            imag = map_imag[half, row, columns, :].astype(jnp.float32)
            yield row, real * value + imag * swap(value)

    def image_side(half, own):
        await_all(half, recv_back, back_recv_sem)
        own.wait()
        copies = []
        for pair in range(2):
            unpack(half, recv_back, -1.0, (2 * pair, 2 * pair + 1), pair == 0)
            for row, term in coil_terms(half, other, pair):
                send_term[half, row] = term.astype(jnp.bfloat16)
                copy = pltpu.make_async_remote_copy(
                    send_term.at[half, row],
                    recv_term.at[half, row],
                    term_send_sem.at[half, row],
                    term_recv_sem.at[half, row],
                    device_id=(me, other),
                    device_id_type=MESH,
                )
                copy.start()
                copies.append(copy)
        for pair in range(2):
            for row, term in coil_terms(half, coil, pair):
                own_term[half, row] = term
        return copies

    first_copies = image_side(0, own2)
    second_copies = image_side(1, own3)
    for halo in halos:
        halo.wait_send()
    for half in range(2):
        await_all(half, send_fwd, fwd_send_sem)
        await_all(half, send_back, back_send_sem)
    tv_store.wait()

    stores = []
    low = low_lanes((HALF, 128))
    for row in range(ROWS):
        first_copies[row].wait()
        second_copies[row].wait()
        first = own_term[0, row] + recv_term[0, row].astype(jnp.float32)
        second = own_term[1, row] + recv_term[1, row].astype(jnp.float32)
        data_part[row, pl.ds(0, HALF, 2), :] = jnp.where(low, first, swap(second))
        data_part[row, pl.ds(1, HALF, 2), :] = jnp.where(low, swap(first), second)
        store = pltpu.make_async_copy(data_part.at[row], data_out.at[row], store_sem.at[row])
        store.start()
        stores.append(store)
    for store in stores:
        store.wait()


def on_device(image_field, coil_maps, samples, kernels, tile_of_block):
    bf16, f32 = jnp.bfloat16, jnp.float32
    dma = pltpu.SemaphoreType.DMA
    hbm = pl.BlockSpec(memory_space=pl.ANY)
    data_part, tv_part = pl.pallas_call(
        body,
        out_shape=[jax.ShapeDtypeStruct((ROWS, 2 * HALF, NZ), f32)] * 2,
        in_specs=[pl.BlockSpec(memory_space=pltpu.VMEM)] + [hbm] * 6,
        out_specs=[hbm] * 2,
        scratch_shapes=[
            pltpu.VMEM((ROWS, 2 * NL, NZ), f32),
            pltpu.VMEM((ROWS, 2 * NL, NZ), bf16),
            pltpu.VMEM((BLOCKS, 256, NZ), bf16),
            pltpu.VMEM((BLOCKS, TILE, TILE), bf16),
            pltpu.VMEM((NL, 2 * NL), bf16),
            pltpu.VMEM((256, 256), bf16),
            pltpu.VMEM((2, ROWS + 2, NL + 2 * PAD, NZ), f32),
            pltpu.VMEM((2, ROWS, NL, NZ), bf16),
            pltpu.VMEM((2, ROWS, NL, NZ), bf16),
            pltpu.VMEM((2, 2 * NL, 4 * 128), bf16),
            pltpu.VMEM((2, PENS, 16, 128), bf16),
            pltpu.VMEM((2, PENS, 16, 128), bf16),
            pltpu.VMEM((2, PENS, 16, 128), bf16),
            pltpu.VMEM((2, PENS, 16, 128), bf16),
            pltpu.VMEM((BLOCKS + 1, TILE, 3 * 128), f32),
            pltpu.VMEM((TILES, TILE, TILE), bf16),
            pltpu.VMEM((2, TILES, TILE, 128), f32),
            pltpu.VMEM((PENS * 16, 128), f32),
            pltpu.VMEM((2, ROWS, HALF, 128), f32),
            pltpu.VMEM((2, ROWS, HALF, 128), bf16),
            pltpu.VMEM((2, ROWS, HALF, 128), bf16),
            pltpu.VMEM((ROWS + 1, 2 * HALF, 128), f32),
            pltpu.VMEM((ROWS, 2 * HALF, 128), f32),
            pltpu.VMEM((2, 2, HALF + 2 * PAD, 128), bf16),
            pltpu.VMEM((2, 2, HALF + 2 * PAD, 128), bf16),
            pltpu.VMEM((2 * BLOCKS, 128), jnp.int32),
            pltpu.SMEM((2 * BLOCKS, 128), jnp.int32),
            dma((6,)),
            dma((4,)),
            dma((2,)),
            dma((2,)),
            dma((2,)),
            dma((2,)),
            dma((2, ROWS)),
            dma((2, ROWS)),
            dma((ROWS + 1,)),
            dma((2,)),
            dma((2,)),
            dma(()),
        ],
        compiler_params=pltpu.CompilerParams(
            collective_id=0, has_side_effects=True, vmem_limit_bytes=56 << 20
        ),
        name="adjoint_gradient",
    )(
        tile_of_block.reshape(1, BLOCKS),
        image_field.reshape(ROWS, 2 * NL, NZ),
        coil_maps.reshape(ROWS, 2 * NL, NZ),
        samples.reshape(BLOCKS, 256, NZ),
        kernels,
        jnp.asarray(dft_table()),
        jnp.asarray(split_table()),
    )
    return (data_part + tv_part).reshape(ROWS, HALF, 2, NZ)


def solution(mesh):
    in_specs = (
        P("pen", None, None, None),
        P("coil", "pen", None, None, None),
        P("coil", "pen", None, None, None),
        P("pen", None, None),
        P("pen"),
    )
    out_specs = P("pen", "coil", None, None)
    return jax.shard_map(
        on_device, mesh=mesh, in_specs=in_specs, out_specs=out_specs, check_vma=False
    )
```
